256 devices in a mesh: dp: 8 (over z_hi, core), row: 4 (over y), col: 8 (over z_lo, x).
Axes of the slice: x: 4, y: 4, z: 8 (z_hi: 4, z_lo: 2; z = z_hi * 2 + z_lo), core: 2. Of those that a mesh axis runs over, the one named last changes fastest.
Arguments:
- tokens: bfloat16 [2048, 8192], P(('dp', 'col'), 'row'), may hold values from -6 to 6
- cotangent: bfloat16 [2048, 8192], P(('dp', 'col'), 'row'), may hold values from -6 to 6
- weight: bfloat16 [8192, 16384], P('row', 'col'), may hold values from -0.125 to 0.125
- block_mask: int32 [32, 64], P('row', 'col'), may hold values 0 or 1
Outputs:
- output: bfloat16 [2048, 8192], P(('dp', 'col'), 'row')
- input_grad: bfloat16 [2048, 8192], P(('dp', 'col'), 'row')
- weight_grad: float32 [8192, 8, 2048], P('row', 'dp', 'col')
The draws below stay inside these ranges and needn't reach their ends.
Inputs may be any that keep to these rules, and one draw needn't show every extreme that they name: block_mask holds only 0 and 1.
All inputs are finite; a program needn't handle non-finite values. No bound on the sum of `block_mask` on one device may be relied on, other than what follows from the above.
Results may differ from the reference program's by a relative error of at most 0.0032.
Values may be sent and summed in bfloat16 or wider, within the bound.
No kernel may reach another device: no remote copies, remote signals or barrier semaphores. Data moves between devices by JAX's collectives and lax.ppermute only.
A program may use at most 128 MiB of HBM per device.

```python
import math
import jax
import jax.numpy as jnp

D = 8192
F = 16384
BLOCK = 256
TOKENS = 2048
N_DP = 8
N_COL = 8


def set_ends(result, key, smallest, high):
    longest = result.shape.index(max(result.shape))
    spots = []
    for shift in (0, 1):
        where = [jax.random.randint(jax.random.fold_in(key, axis), (), 0, length) for axis, length in enumerate(result.shape)]
        where[longest] = (where[longest] + shift) % result.shape[longest]
        spots.append(tuple(where))
    return result.at[spots[0]].set(smallest).at[spots[1]].set(high)


def block_levels(key, extent, split, least, top_value):
    def one(axis_at, parts):
        draws = jax.random.uniform(jax.random.fold_in(jax.random.fold_in(key, 6), axis_at), (parts,), jnp.float32, least / len(split), top_value / len(split))
        return jnp.repeat(jnp.exp(draws), extent[axis_at] // parts).reshape((-1,) + (1,) * (len(extent) - axis_at - 1))

    level = one(*split[0])
    for cut in split[1:]:
        level = level * one(*cut)
    return level


def normal_values(stream_key, shape, width, bound, split=(), kind=jnp.bfloat16):
    result = width * jax.random.normal(stream_key, shape, jnp.float32)
    if split:
        result = result * block_levels(stream_key, shape, split, -0.22, 0.18)
    return jnp.clip(result, -bound, bound).astype(kind)


def setup_inputs(seed: int = 0) -> dict:
    seeds = jax.random.split(jax.random.key(seed), 5)
    tokens = normal_values(seeds[0], (TOKENS, D), 1.0, 6.0, ((0, 64), (1, 4)))
    cotangent = normal_values(seeds[1], (TOKENS, D), 1.0, 6.0, ((0, 64), (1, 4)))
    weight = normal_values(seeds[2], (D, F), (D // 4) ** -0.5, 0.125, ((0, 4), (1, 8)))
    block_mask = set_ends((jax.random.randint(seeds[3], (D // BLOCK, F // BLOCK), 0, 4) < 1).astype(jnp.int32), jax.random.fold_in(seeds[3], 1), 0, 1)
    return dict(tokens=tokens, cotangent=cotangent, weight=weight, block_mask=block_mask)


def expand_mask(block_mask):
    kept_blocks = block_mask.astype(jnp.bfloat16)
    return jnp.repeat(jnp.repeat(kept_blocks, BLOCK, axis=0), BLOCK, axis=1)

def reference(tokens, cotangent, weight, block_mask):
    kept = expand_mask(block_mask)
    masked = weight * kept
    pre = jnp.dot(tokens, masked, preferred_element_type=jnp.float32)
    hidden = jax.nn.silu(pre).astype(jnp.bfloat16)
    projected = jnp.dot(hidden, masked.T, preferred_element_type=jnp.float32)
    output = (tokens.astype(jnp.float32) + projected).astype(jnp.bfloat16)
    grad_hidden = jnp.dot(cotangent, masked, preferred_element_type=jnp.float32)
    sigmoid_pre = jax.nn.sigmoid(pre)
    grad_pre = (grad_hidden * sigmoid_pre * (1.0 + pre * (1.0 - sigmoid_pre))).astype(jnp.bfloat16)
    back = jnp.dot(grad_pre, masked.T, preferred_element_type=jnp.float32)
    input_grad = (cotangent.astype(jnp.float32) + back).astype(jnp.bfloat16)
    full = jnp.dot(cotangent.T, hidden, preferred_element_type=jnp.float32)
    full = full + jnp.dot(tokens.T, grad_pre, preferred_element_type=jnp.float32)
    full = full * kept.astype(jnp.float32) * (1.0 / math.sqrt(TOKENS))
    share_cols = F // (N_COL * N_DP)
    weight_grad = full.reshape(D, N_COL, N_DP, share_cols).transpose(0, 2, 1, 3).reshape(D, N_DP, N_COL * share_cols)
    return (output, input_grad, weight_grad)
```

```python
import functools
import math

import jax
import jax.numpy as jnp
from jax import lax
from jax.experimental import pallas as pl
from jax.experimental.pallas import tpu as pltpu
from jax.sharding import PartitionSpec as P

BLOCK = 256
VMEM_LIMIT = 56 * 1024 * 1024
SMEM_SPEC = pl.BlockSpec(memory_space=pltpu.SMEM)
BF16, F32 = jnp.bfloat16, jnp.float32


def shift(value, axis, by):
    size = lax.axis_size(axis)
    return lax.ppermute(value, axis, [(i, (i + by) % size) for i in range(size)])


def params(steps=1):
    return pltpu.CompilerParams(
        vmem_limit_bytes=VMEM_LIMIT, dimension_semantics=("arbitrary",) * steps
    )


def masked_copy(mask_ref, w_ref, out_ref, row0, col0):
    for i in range(w_ref.shape[0] // BLOCK):
        for j in range(w_ref.shape[1] // BLOCK):
            part = (pl.ds(i * BLOCK, BLOCK), pl.ds(j * BLOCK, BLOCK))
            kept = mask_ref[row0 + i, col0 + j] != 0
            out_ref[part] = jnp.where(kept, w_ref[part], jnp.zeros((BLOCK, BLOCK), BF16))


def up_kernel(n_col, n_row, pos_ref, mask_ref, *refs):
    parts, w_ref = refs[:n_col], refs[n_col]
    own_ref, sends = refs[n_col + 1], refs[n_col + 2 : n_col + 1 + n_row]
    x_ref, wm_ref, acc_ref = refs[-3:]
    rows = parts[0].shape[1]
    tok = rows * n_col
    step = pl.program_id(0)

    @pl.when(step == 0)
    def _():
        for t in range(2):
            for j in range(n_col):
                x_ref[pl.ds(t * tok + j * rows, rows), :] = parts[j][t]

    masked_copy(mask_ref, w_ref, wm_ref, 0, step * (w_ref.shape[1] // BLOCK))
    acc_ref[...] = jnp.dot(x_ref[...], wm_ref[...], preferred_element_type=F32)
    share = tok // n_row
    me = pos_ref[0]
    for t in range(2):
        for k in range(n_row):
            first = pl.multiple_of(t * tok + lax.rem(me + k, n_row) * share, share)
            value = acc_ref[pl.ds(first, share), :]
            if k == 0:
                own_ref[t] = value
            else:
                sends[k - 1][t] = value.astype(BF16)


def up(pos, mask, parts, weight, n_row, width=512):
    n_col, (_, rows, depth) = len(parts), parts[0].shape
    cols = weight.shape[1]
    tok = rows * n_col
    share = tok // n_row
    return pl.pallas_call(
        functools.partial(up_kernel, n_col, n_row),
        grid=(cols // width,),
        in_specs=[SMEM_SPEC, SMEM_SPEC]
        + [pl.BlockSpec((2, rows, depth), lambda n: (0, 0, 0))] * n_col
        + [pl.BlockSpec((depth, width), lambda n: (0, n))],
        out_specs=[pl.BlockSpec((2, share, width), lambda n: (0, 0, n))] * n_row,
        out_shape=[jax.ShapeDtypeStruct((2, share, cols), F32)]
        + [jax.ShapeDtypeStruct((2, share, cols), BF16)] * (n_row - 1),
        scratch_shapes=[
            pltpu.VMEM((2 * tok, depth), BF16),
            pltpu.VMEM((depth, width), BF16),
            pltpu.VMEM((2 * tok, width), F32),
        ],
        compiler_params=params(),
        name="up",
    )(pos, mask, *parts, weight)


def act_kernel(n_row, n_z, pos_ref, *refs):
    own_ref, recv = refs[0], refs[1:n_row]
    both_ref, pieces = refs[n_row], refs[n_row + 1 :]
    pre = own_ref[0]
    grad_hidden = own_ref[1]
    for ref in recv:
        pre = pre + ref[0].astype(F32)
        grad_hidden = grad_hidden + ref[1].astype(F32)
    sig = jax.nn.sigmoid(pre)
    both_ref[0] = (pre * sig).astype(BF16)
    both_ref[1] = (grad_hidden * sig * (1.0 + pre * (1.0 - sig))).astype(BF16)
    width = both_ref.shape[2] // n_z
    for k in range(n_z):
        first = pl.multiple_of(lax.rem(pos_ref[1] + k, n_z) * width, width)
        for t in range(2):
            pieces[k][t] = both_ref[t, :, pl.ds(first, width)]


def act(pos, own, recv, n_z):
    _, share, cols = own.shape
    return pl.pallas_call(
        functools.partial(act_kernel, len(recv) + 1, n_z),
        in_specs=[SMEM_SPEC] + [pl.BlockSpec(memory_space=pltpu.VMEM)] * (len(recv) + 1),
        out_specs=[pl.BlockSpec(memory_space=pltpu.VMEM)] * (n_z + 1),
        out_shape=[jax.ShapeDtypeStruct((2, share, cols), BF16)]
        + [jax.ShapeDtypeStruct((2, share, cols // n_z), BF16)] * n_z,
        compiler_params=params(0),
        name="act",
    )(pos, own, *recv)


def down_kernel(n_col, n_row, pos_ref, mask_ref, *refs):
    parts, w_ref = refs[:n_row], refs[n_row]
    own_ref, sends = refs[n_row + 1], refs[n_row + 2 : n_row + 1 + n_col]
    x_ref, wm_ref, acc_ref = refs[-3:]
    share = parts[0].shape[1]
    tok = share * n_row
    step = pl.program_id(0)

    @pl.when(step == 0)
    def _():
        for t in range(2):
            for k in range(n_row):
                owner = lax.rem(pos_ref[0] + n_row - k, n_row)
                first = pl.multiple_of(t * tok + owner * share, share)
                x_ref[pl.ds(first, share), :] = parts[k][t]

    masked_copy(mask_ref, w_ref, wm_ref, step * (w_ref.shape[0] // BLOCK), 0)
    acc_ref[...] = lax.dot_general(
        x_ref[...], wm_ref[...], (((1,), (1,)), ((), ())), preferred_element_type=F32
    )
    rows = tok // n_col
    for t in range(2):
        own_ref[t] = acc_ref[pl.ds(t * tok, rows), :]
        for j in range(1, n_col):
            sends[j - 1][t] = acc_ref[pl.ds(t * tok + j * rows, rows), :].astype(BF16)


def down(pos, mask, parts, weight, n_col, width=512):
    n_row, (_, share, depth) = len(parts), parts[0].shape
    feats = weight.shape[0]
    tok = share * n_row
    rows = tok // n_col
    return pl.pallas_call(
        functools.partial(down_kernel, n_col, n_row),
        grid=(feats // width,),
        in_specs=[SMEM_SPEC, SMEM_SPEC]
        + [pl.BlockSpec((2, share, depth), lambda n: (0, 0, 0))] * n_row
        + [pl.BlockSpec((width, depth), lambda n: (n, 0))],
        out_specs=[pl.BlockSpec((2, rows, width), lambda n: (0, 0, n))] * n_col,
        out_shape=[jax.ShapeDtypeStruct((2, rows, feats), F32)]
        + [jax.ShapeDtypeStruct((2, rows, feats), BF16)] * (n_col - 1),
        scratch_shapes=[
            pltpu.VMEM((2 * tok, depth), BF16),
            pltpu.VMEM((width, depth), BF16),
            pltpu.VMEM((2 * tok, width), F32),
        ],
        compiler_params=params(),
        name="down",
    )(pos, mask, *parts, weight)


def grad_kernel(n_col, n_row, n_z, half, pos_ref, *refs):
    near, far = refs[:n_col], refs[n_col : 2 * n_col]
    hidden = refs[2 * n_col : 2 * n_col + n_row]
    out_ref, x_ref, h_ref = refs[-3:]
    rows = near[0].shape[1]
    share = hidden[0].shape[2]
    tok = rows * n_col

    @pl.when(pl.program_id(0) == 0)
    def _():
        side = pos_ref[2] if half == 0 else 1 - pos_ref[2]
        first_col = pl.multiple_of(side * BLOCK, BLOCK)
        for k in range(n_row):
            owner = lax.rem(pos_ref[0] + n_row - k, n_row)
            for z in range(n_z):
                first = pl.multiple_of(z * tok + owner * share, share)
                for t in range(2):
                    h_ref[t, pl.ds(first, share), :] = hidden[k][z, t, :, pl.ds(first_col, BLOCK)]

    for t in range(2):
        for j in range(n_col):
            x_ref[t, pl.ds(j * rows, rows), :] = near[j][t]
            for z in range(1, n_z):
                x_ref[t, pl.ds(z * tok + j * rows, rows), :] = far[j][z - 1, t]
    over_tokens = (((0,), (0,)), ((), ()))
    total = lax.dot_general(x_ref[1], h_ref[0], over_tokens, preferred_element_type=F32)
    total += lax.dot_general(x_ref[0], h_ref[1], over_tokens, preferred_element_type=F32)
    out_ref[...] = total


def grad(pos, near, far, hidden, half, width=512):
    n_col, n_row = len(near), len(hidden)
    _, rows, feats = near[0].shape
    n_z, _, share, cols = hidden[0].shape
    tok = n_z * rows * n_col
    return pl.pallas_call(
        functools.partial(grad_kernel, n_col, n_row, n_z, half),
        grid=(feats // width,),
        in_specs=[SMEM_SPEC]
        + [pl.BlockSpec((2, rows, width), lambda n: (0, 0, n))] * n_col
        + [pl.BlockSpec((n_z - 1, 2, rows, width), lambda n: (0, 0, 0, n))] * n_col
        + [pl.BlockSpec((n_z, 2, share, cols), lambda n: (0, 0, 0, 0))] * n_row,
        out_specs=pl.BlockSpec((width, BLOCK), lambda n: (n, 0)),
        out_shape=jax.ShapeDtypeStruct((feats, BLOCK), F32),
        scratch_shapes=[pltpu.VMEM((2, tok, width), BF16), pltpu.VMEM((2, tok, BLOCK), BF16)],
        compiler_params=params(),
        name="grad",
    )(pos, *near, *far, *hidden)


def finish_kernel(norm_scale, pos_ref, mask_ref, a_ref, b_ref, out_ref):
    rows = a_ref.shape[0]
    kept = mask_ref[pl.program_id(0), pos_ref[3]] != 0
    total = (a_ref[...] + b_ref[...]) * norm_scale
    total = jnp.where(kept, total, jnp.zeros_like(total))
    out_ref[pl.ds(0, rows, 2), :] = total[:, :128]
    out_ref[pl.ds(1, rows, 2), :] = total[:, 128:]


def finish(pos, mask, mine, theirs, norm_scale):
    feats = mine.shape[0]
    block = pl.BlockSpec((BLOCK, BLOCK), lambda n: (n, 0))
    return pl.pallas_call(
        functools.partial(finish_kernel, norm_scale),
        grid=(feats // BLOCK,),
        in_specs=[SMEM_SPEC, SMEM_SPEC, block, block],
        out_specs=pl.BlockSpec((2 * BLOCK, 128), lambda n: (n, 0)),
        out_shape=jax.ShapeDtypeStruct((2 * feats, 128), F32),
        compiler_params=params(),
        name="finish",
    )(pos, mask, mine, theirs)


def on_device(tokens, cotangent, weight, block_mask):
    n_dp, n_row, n_col = (lax.axis_size(a) for a in ("dp", "row", "col"))
    n_z = n_dp // 2
    dp_at = lax.axis_index("dp")
    pos = jnp.stack([lax.axis_index("row"), dp_at // 2, dp_at % 2, dp_at]).astype(jnp.int32)
    both = jnp.stack([tokens, cotangent])

    near = [both] + [shift(both, "col", j) for j in range(1, n_col)]
    far0 = jnp.stack([shift(both, "dp", 2 * k) for k in range(1, n_z)])

    own, *sends = up(pos, block_mask, near, weight, n_row)
    recv = [shift(s, "row", k + 1) for k, s in enumerate(sends)]
    far = [far0] + [shift(far0, "col", j) for j in range(1, n_col)]
    acts, *pieces = act(pos, own, recv, n_z)
    acts_all = [acts] + [shift(acts, "row", k) for k in range(1, n_row)]
    pieces = jnp.stack([pieces[0]] + [shift(pieces[k], "dp", 2 * k) for k in range(1, n_z)])
    pieces_all = [pieces] + [shift(pieces, "row", k) for k in range(1, n_row)]

    own, *sends = down(pos, block_mask, acts_all, weight, n_col)
    total = own + both.astype(F32)
    for j, s in enumerate(sends):
        total = total + shift(s, "col", -(j + 1)).astype(F32)
    output, input_grad = total[0].astype(BF16), total[1].astype(BF16)

    given = grad(pos, near, far, pieces_all, 1)
    theirs = lax.ppermute(given, "dp", [(i, i ^ 1) for i in range(n_dp)])
    mine = grad(pos, near, far, pieces_all, 0)
    tok_total = tokens.shape[0] * n_col * n_dp
    weight_grad = finish(pos, block_mask, mine, theirs, 1.0 / math.sqrt(tok_total))
    return output, input_grad, weight_grad.reshape(weight.shape[0], 1, BLOCK)


def solution(mesh):
    in_specs = (P(("dp", "col"), "row"), P(("dp", "col"), "row"), P("row", "col"), P("row", "col"))
    out_specs = (P(("dp", "col"), "row"), P(("dp", "col"), "row"), P("row", "dp", "col"))
    return jax.shard_map(
        on_device, mesh=mesh, in_specs=in_specs, out_specs=out_specs, check_vma=False
    )
```

```python
import functools
import math

import jax
import jax.numpy as jnp
from jax import lax
from jax.experimental import pallas as pl
from jax.experimental.pallas import tpu as pltpu
from jax.sharding import PartitionSpec as P

BLOCK = 256
VMEM_LIMIT = 56 * 1024 * 1024
SMEM_SPEC = pl.BlockSpec(memory_space=pltpu.SMEM)
COST = pl.CostEstimate(flops=1, bytes_accessed=1, transcendentals=0)
BF16, F32 = jnp.bfloat16, jnp.float32


def shift(value, axis, by):
    size = lax.axis_size(axis)
    return lax.ppermute(value, axis, [(i, (i + by) % size) for i in range(size)])


def shift_col(value, by_x, swap=0):
    half = lax.axis_size("col") // 2
    pairs = [(i, (i // half ^ swap) * half + (i + by_x) % half) for i in range(2 * half)]
    return lax.ppermute(value, "col", pairs)


def params(steps=1):
    return pltpu.CompilerParams(
        vmem_limit_bytes=VMEM_LIMIT, dimension_semantics=("arbitrary",) * steps
    )


def masked_copy(mask_ref, w_ref, out_ref, row0, col0):
    for i in range(w_ref.shape[0] // BLOCK):
        for j in range(w_ref.shape[1] // BLOCK):
            part = (pl.ds(i * BLOCK, BLOCK), pl.ds(j * BLOCK, BLOCK))
            kept = mask_ref[row0 + i, col0 + j] != 0
            out_ref[part] = jnp.where(kept, w_ref[part], jnp.zeros((BLOCK, BLOCK), BF16))


def up_kernel(n_col, n_row, pos_ref, mask_ref, *refs):
    parts, w_ref = refs[:n_col], refs[n_col]
    own_ref, sends = refs[n_col + 1], refs[n_col + 2 : n_col + 1 + n_row]
    x_ref, wm_ref, acc_ref = refs[-3:]
    rows = parts[0].shape[2]
    tok = rows * 2 * n_col
    step = pl.program_id(0)

    @pl.when(step == 0)
    def _():
        for t in range(2):
            for j in range(n_col):
                for side in range(2):
                    x_ref[pl.ds(t * tok + (2 * j + side) * rows, rows), :] = parts[j][side, t]

    masked_copy(mask_ref, w_ref, wm_ref, 0, step * (w_ref.shape[1] // BLOCK))
    acc_ref[...] = jnp.dot(x_ref[...], wm_ref[...], preferred_element_type=F32)
    share = tok // n_row
    me = pos_ref[0]
    for t in range(2):
        for k in range(n_row):
            first = pl.multiple_of(t * tok + lax.rem(me + k, n_row) * share, share)
            value = acc_ref[pl.ds(first, share), :]
            if k == 0:
                own_ref[t] = value
            else:
                sends[k - 1][t] = value.astype(BF16)


def up(pos, mask, parts, weight, n_row, width=512):
    n_col, (_, _, rows, depth) = len(parts), parts[0].shape
    cols = weight.shape[1]
    tok = rows * 2 * n_col
    share = tok // n_row
    return pl.pallas_call(
        functools.partial(up_kernel, n_col, n_row),
        grid=(cols // width,),
        in_specs=[SMEM_SPEC, SMEM_SPEC]
        + [pl.BlockSpec((2, 2, rows, depth), lambda n: (0, 0, 0, 0))] * n_col
        + [pl.BlockSpec((depth, width), lambda n: (0, n))],
        out_specs=[pl.BlockSpec((2, share, width), lambda n: (0, 0, n))] * n_row,
        out_shape=[jax.ShapeDtypeStruct((2, share, cols), F32)]
        + [jax.ShapeDtypeStruct((2, share, cols), BF16)] * (n_row - 1),
        scratch_shapes=[
            pltpu.VMEM((2 * tok, depth), BF16),
            pltpu.VMEM((depth, width), BF16),
            pltpu.VMEM((2 * tok, width), F32),
        ],
        cost_estimate=COST,
        compiler_params=params(),
        name="up",
    )(pos, mask, *parts, weight)


def act_kernel(n_row, *refs):
    own_ref, recv = refs[0], refs[1:n_row]
    both_ref = refs[n_row]
    pre = own_ref[0]
    grad_hidden = own_ref[1]
    for ref in recv:
        pre = pre + ref[0].astype(F32)
        grad_hidden = grad_hidden + ref[1].astype(F32)
    sig = jax.nn.sigmoid(pre)
    both_ref[0] = (pre * sig).astype(BF16)
    both_ref[1] = (grad_hidden * sig * (1.0 + pre * (1.0 - sig))).astype(BF16)


def act(own, recv):
    _, share, cols = own.shape
    return pl.pallas_call(
        functools.partial(act_kernel, len(recv) + 1),
        in_specs=[pl.BlockSpec(memory_space=pltpu.VMEM)] * (len(recv) + 1),
        out_specs=pl.BlockSpec(memory_space=pltpu.VMEM),
        out_shape=jax.ShapeDtypeStruct((2, share, cols), BF16),
        cost_estimate=COST,
        compiler_params=params(0),
        name="act",
    )(own, *recv)


def down_kernel(n_col, n_row, pos_ref, mask_ref, *refs):
    parts, w_ref, send_ref = refs[:n_row], refs[n_row], refs[n_row + 1]
    x_ref, wm_ref, acc_ref = refs[-3:]
    share = parts[0].shape[1]
    tok = share * n_row
    step = pl.program_id(0)

    @pl.when(step == 0)
    def _():
        for t in range(2):
            for k in range(n_row):
                owner = lax.rem(pos_ref[0] + n_row - k, n_row)
                first = pl.multiple_of(t * tok + owner * share, share)
                x_ref[pl.ds(first, share), :] = parts[k][t]

    masked_copy(mask_ref, w_ref, wm_ref, step * (w_ref.shape[0] // BLOCK), 0)
    acc_ref[...] = lax.dot_general(
        x_ref[...], wm_ref[...], (((1,), (1,)), ((), ())), preferred_element_type=F32
    )
    rows = tok // n_col
    n_x = n_col // 2
    for j in range(n_x):
        for side in range(2):
            to_z = pos_ref[5] if side == 0 else 1 - pos_ref[5]
            to = to_z * n_x + lax.rem(pos_ref[4] + n_x - j, n_x)
            for t in range(2):
                first = t * tok + (2 * j + side) * rows
                send_ref[to, t] = acc_ref[pl.ds(first, rows), :].astype(BF16)


def down(pos, mask, parts, weight, n_col, width=512):
    n_row, (_, share, depth) = len(parts), parts[0].shape
    feats = weight.shape[0]
    tok = share * n_row
    rows = tok // n_col
    return pl.pallas_call(
        functools.partial(down_kernel, n_col, n_row),
        grid=(feats // width,),
        in_specs=[SMEM_SPEC, SMEM_SPEC]
        + [pl.BlockSpec((2, share, depth), lambda n: (0, 0, 0))] * n_row
        + [pl.BlockSpec((width, depth), lambda n: (n, 0))],
        out_specs=pl.BlockSpec((n_col, 2, rows, width), lambda n: (0, 0, 0, n)),
        out_shape=jax.ShapeDtypeStruct((n_col, 2, rows, feats), BF16),
        scratch_shapes=[
            pltpu.VMEM((2 * tok, depth), BF16),
            pltpu.VMEM((width, depth), BF16),
            pltpu.VMEM((2 * tok, width), F32),
        ],
        cost_estimate=COST,
        compiler_params=params(),
        name="down",
    )(pos, mask, *parts, weight)


def grad_kernel(n_col, n_row, n_z, pos_ref, *refs):
    near, far = refs[:n_col], refs[n_col : 2 * n_col + 1]
    hidden = refs[2 * n_col + 1 : 2 * n_col + 1 + n_row]
    mine_ref, other_ref, x_ref, h_ref, sum_ref = refs[-5:]
    rows = near[0].shape[2]
    share = hidden[0].shape[2]
    tok = rows * 2 * n_col

    @pl.when(pl.program_id(0) == 0)
    def _():
        for k in range(n_row):
            owner = lax.rem(pos_ref[0] + n_row - k, n_row)
            for z in range(n_z):
                behind = lax.rem(pos_ref[1] + n_z - z, n_z)
                first = pl.multiple_of(behind * tok + owner * share, share)
                for t in range(2):
                    h_ref[t, pl.ds(first, share), :] = hidden[k][z, t]

    for t in range(2):
        for j in range(n_col):
            for side in range(2):
                first = (2 * j + side) * rows
                x_ref[t, pl.ds(first, rows), :] = near[j][side, t]
                source = far[n_col if j == 2 and side == 1 else j]
                for z in range(1, n_z):
                    at = 0 if j == 2 else side
                    x_ref[t, pl.ds(z * tok + first, rows), :] = source[at, z - 1, t]
    over_tokens = (((0,), (0,)), ((), ()))
    total = lax.dot_general(x_ref[1], h_ref[0], over_tokens, preferred_element_type=F32)
    total += lax.dot_general(x_ref[0], h_ref[1], over_tokens, preferred_element_type=F32)
    sum_ref[...] = total
    mine = pl.multiple_of(pos_ref[2] * BLOCK, BLOCK)
    mine_ref[...] = sum_ref[:, pl.ds(mine, BLOCK)]
    other_ref[...] = sum_ref[:, pl.ds(BLOCK - mine, BLOCK)]


def grad(pos, near, far, hidden, width=512):
    n_col, n_row = len(near), len(hidden)
    _, _, rows, feats = near[0].shape
    n_z, _, share, cols = hidden[0].shape
    tok = n_z * rows * 2 * n_col
    return pl.pallas_call(
        functools.partial(grad_kernel, n_col, n_row, n_z),
        grid=(feats // width,),
        in_specs=[SMEM_SPEC]
        + [pl.BlockSpec((2, 2, rows, width), lambda n: (0, 0, 0, n))] * n_col
        + [
            pl.BlockSpec((f.shape[0], n_z - 1, 2, rows, width), lambda n: (0, 0, 0, 0, n))
            for f in far
        ]
        + [pl.BlockSpec((n_z, 2, share, cols), lambda n: (0, 0, 0, 0))] * n_row,
        out_specs=[pl.BlockSpec((width, BLOCK), lambda n: (n, 0))] * 2,
        out_shape=[jax.ShapeDtypeStruct((feats, BLOCK), F32)] * 2,
        scratch_shapes=[
            pltpu.VMEM((2, tok, width), BF16),
            pltpu.VMEM((2, tok, cols), BF16),
            pltpu.VMEM((width, cols), F32),
        ],
        cost_estimate=COST,
        compiler_params=params(),
        name="grad",
    )(pos, *near, *far, *hidden)


def finish_kernel(norm_scale, pos_ref, mask_ref, a_ref, b_ref, out_ref):
    blocks = a_ref.shape[0] // BLOCK
    for i in range(blocks):
        kept = mask_ref[pl.program_id(0) * blocks + i, pos_ref[3]] != 0
        part = pl.ds(i * BLOCK, BLOCK)
        total = (a_ref[part, :] + b_ref[part, :]) * norm_scale
        total = jnp.where(kept, total, jnp.zeros_like(total))
        out_ref[pl.ds(2 * i * BLOCK, BLOCK, 2), :] = total[:, :128]
        out_ref[pl.ds(2 * i * BLOCK + 1, BLOCK, 2), :] = total[:, 128:]


def finish(pos, mask, mine, theirs, norm_scale, height=1024):
    feats = mine.shape[0]
    block = pl.BlockSpec((height, BLOCK), lambda n: (n, 0))
    return pl.pallas_call(
        functools.partial(finish_kernel, norm_scale),
        grid=(feats // height,),
        in_specs=[SMEM_SPEC, SMEM_SPEC, block, block],
        out_specs=pl.BlockSpec((2 * height, 128), lambda n: (n, 0)),
        out_shape=jax.ShapeDtypeStruct((2 * feats, 128), F32),
        cost_estimate=COST,
        compiler_params=params(),
        name="finish",
    )(pos, mask, mine, theirs)


def on_device(tokens, cotangent, weight, block_mask):
    n_dp, n_row, n_col = (lax.axis_size(a) for a in ("dp", "row", "col"))
    n_z = n_dp // 2
    n_x = n_col // 2
    dp_at, col_at = lax.axis_index("dp"), lax.axis_index("col")
    pos = jnp.stack(
        [lax.axis_index("row"), dp_at // 2, dp_at % 2, dp_at, col_at % n_x, col_at // n_x]
    ).astype(jnp.int32)
    both = jnp.stack([tokens, cotangent])

    pair = jnp.stack([both, shift_col(both, 0, 1)])
    near = [pair] + [shift_col(pair, j) for j in range(1, n_x)]
    far = [shift(pair, "dp", 2 * k) for k in range(1, n_z)]

    own, *sends = up(pos, block_mask, near, weight, n_row)
    recv = [shift(s, "row", k + 1) for k, s in enumerate(sends)]
    own, recv, far = lax.optimization_barrier((own, recv, far))
    far = jnp.stack(far, axis=1)
    left, right = shift_col(far, 1), shift_col(far, -1)
    z_groups = [list(range(c, n_dp, 2)) for c in range(2)]
    acts = act(own, recv)
    acts_all = [acts] + [shift(acts, "row", k) for k in range(1, n_row)]
    pieces = acts.reshape(2, acts.shape[1], n_z, -1).transpose(2, 0, 1, 3)
    pieces = lax.all_to_all(pieces, "dp", 0, 0, axis_index_groups=z_groups)
    acts_all, pieces, left, right = lax.optimization_barrier((acts_all, pieces, left, right))
    pieces_all = [pieces] + [shift(pieces, "row", k) for k in range(1, n_row)]
    across = [shift_col(left[:1], 1), shift_col(right[1:], -1)]
    far = [far, left, across[0], right, across[1]]

    sends = down(pos, block_mask, acts_all, weight, n_col)
    sends, near = lax.optimization_barrier((sends, near))
    total = lax.all_to_all(sends, "col", 0, 0).astype(F32).sum(axis=0) + both.astype(F32)
    output, input_grad = total[0].astype(BF16), total[1].astype(BF16)

    mine, given = grad(pos, near, far, pieces_all)
    theirs = lax.ppermute(given, "dp", [(i, i ^ 1) for i in range(n_dp)])
    tok_total = tokens.shape[0] * n_col * n_dp
    weight_grad = finish(pos, block_mask, mine, theirs, 1.0 / math.sqrt(tok_total))
    return output, input_grad, weight_grad.reshape(weight.shape[0], 1, BLOCK)


def solution(mesh):
    in_specs = (P(("dp", "col"), "row"), P(("dp", "col"), "row"), P("row", "col"), P("row", "col"))
    out_specs = (P(("dp", "col"), "row"), P(("dp", "col"), "row"), P("row", "dp", "col"))
    return jax.shard_map(
        on_device, mesh=mesh, in_specs=in_specs, out_specs=out_specs, check_vma=False
    )
```

```python
import functools
import math

import jax
import jax.numpy as jnp
from jax import lax
from jax.experimental import pallas as pl
from jax.experimental.pallas import tpu as pltpu
from jax.sharding import PartitionSpec as P

BLOCK = 256
VMEM_LIMIT = 24 * 1024 * 1024
WIDE_LIMIT = 56 * 1024 * 1024
SMEM_SPEC = pl.BlockSpec(memory_space=pltpu.SMEM)
COST = pl.CostEstimate(flops=1, bytes_accessed=1, transcendentals=0)
LONG = pl.CostEstimate(flops=100000000000, bytes_accessed=1000000000, transcendentals=0)
BF16, F32 = jnp.bfloat16, jnp.float32


def shift(value, axis, by):
    size = lax.axis_size(axis)
    return lax.ppermute(value, axis, [(i, (i + by) % size) for i in range(size)])


def shift_col(value, by_x, swap=0):
    half = lax.axis_size("col") // 2
    pairs = [(i, (i // half ^ swap) * half + (i + by_x) % half) for i in range(2 * half)]
    return lax.ppermute(value, "col", pairs)


def params(steps=1, limit=VMEM_LIMIT):
    return pltpu.CompilerParams(
        vmem_limit_bytes=limit, dimension_semantics=("arbitrary",) * steps
    )


def masked_copy(mask_ref, w_ref, out_ref, row0, col0):
    for i in range(w_ref.shape[0] // BLOCK):
        for j in range(w_ref.shape[1] // BLOCK):
            part = (pl.ds(i * BLOCK, BLOCK), pl.ds(j * BLOCK, BLOCK))
            kept = mask_ref[row0 + i, col0 + j] != 0
            out_ref[part] = jnp.where(kept, w_ref[part], jnp.zeros((BLOCK, BLOCK), BF16))


def up_kernel(n_col, n_row, pos_ref, mask_ref, *refs):
    parts, w_ref = refs[:n_col], refs[n_col]
    own_ref, sends = refs[n_col + 1], refs[n_col + 2 : n_col + 1 + n_row]
    x_ref, wm_ref, acc_ref = refs[-3:]
    rows = parts[0].shape[2]
    tok = rows * 2 * n_col
    step = pl.program_id(0)

    @pl.when(step == 0)
    def _():
        for t in range(2):
            for j in range(n_col):
                for side in range(2):
                    x_ref[pl.ds(t * tok + (2 * j + side) * rows, rows), :] = parts[j][side, t]

    masked_copy(mask_ref, w_ref, wm_ref, 0, step * (w_ref.shape[1] // BLOCK))
    acc_ref[...] = jnp.dot(x_ref[...], wm_ref[...], preferred_element_type=F32)
    share = tok // n_row
    me = pos_ref[0]
    for t in range(2):
        for k in range(n_row):
            first = pl.multiple_of(t * tok + lax.rem(me + k, n_row) * share, share)
            value = acc_ref[pl.ds(first, share), :]
            if k == 0:
                own_ref[t] = value
            else:
                sends[k - 1][t] = value.astype(BF16)


def up(pos, mask, parts, weight, n_row, width=512):
    n_col, (_, _, rows, depth) = len(parts), parts[0].shape
    cols = weight.shape[1]
    tok = rows * 2 * n_col
    share = tok // n_row
    return pl.pallas_call(
        functools.partial(up_kernel, n_col, n_row),
        grid=(cols // width,),
        in_specs=[SMEM_SPEC, SMEM_SPEC]
        + [pl.BlockSpec((2, 2, rows, depth), lambda n: (0, 0, 0, 0))] * n_col
        + [pl.BlockSpec((depth, width), lambda n: (0, n))],
        out_specs=[pl.BlockSpec((2, share, width), lambda n: (0, 0, n))] * n_row,
        out_shape=[jax.ShapeDtypeStruct((2, share, cols), F32)]
        + [jax.ShapeDtypeStruct((2, share, cols), BF16)] * (n_row - 1),
        scratch_shapes=[
            pltpu.VMEM((2 * tok, depth), BF16),
            pltpu.VMEM((depth, width), BF16),
            pltpu.VMEM((2 * tok, width), F32),
        ],
        cost_estimate=COST,
        compiler_params=params(),
        name="up",
    )(pos, mask, *parts, pltpu.with_memory_space_constraint(weight, pltpu.HBM))


def act_kernel(n_row, n_z, pos_ref, *refs):
    own_ref, recv = refs[0], refs[1:n_row]
    all_ref, pieces = refs[n_row], refs[n_row + 1 :]
    pre = own_ref[0]
    grad_hidden = own_ref[1]
    for ref in recv:
        pre = pre + ref[0].astype(F32)
        grad_hidden = grad_hidden + ref[1].astype(F32)
    sig = jax.nn.sigmoid(pre)
    all_ref[0, 0] = (pre * sig).astype(BF16)
    all_ref[0, 1] = (grad_hidden * sig * (1.0 + pre * (1.0 - sig))).astype(BF16)
    for r in range(1, n_row):
        all_ref[r] = all_ref[0]
    width = all_ref.shape[3] // n_z
    for k in range(n_z):
        first = pl.multiple_of(lax.rem(pos_ref[1] + k, n_z) * width, width)
        pieces[k][...] = all_ref[0, :, :, pl.ds(first, width)]


def act(pos, own, recv, n_z):
    _, share, cols = own.shape
    n_row = len(recv) + 1
    return pl.pallas_call(
        functools.partial(act_kernel, n_row, n_z),
        in_specs=[SMEM_SPEC] + [pl.BlockSpec(memory_space=pltpu.VMEM)] * n_row,
        out_specs=[pl.BlockSpec(memory_space=pltpu.VMEM)] * (n_z + 1),
        out_shape=[jax.ShapeDtypeStruct((n_row, 2, share, cols), BF16)]
        + [jax.ShapeDtypeStruct((2, share, cols // n_z), BF16)] * n_z,
        cost_estimate=COST,
        compiler_params=params(0),
        name="act",
    )(pos, own, *recv)


def down_kernel(n_col, n_row, pos_ref, mask_ref, *refs):
    parts_ref, w_ref, send_ref = refs[:3]
    x_ref, wm_ref, acc_ref = refs[-3:]
    share = parts_ref.shape[2]
    tok = share * n_row
    step = pl.program_id(0)

    @pl.when(step == 0)
    def _():
        for t in range(2):
            for r in range(n_row):
                x_ref[pl.ds(t * tok + r * share, share), :] = parts_ref[r, t]

    masked_copy(mask_ref, w_ref, wm_ref, step * (w_ref.shape[0] // BLOCK), 0)
    acc_ref[...] = lax.dot_general(
        x_ref[...], wm_ref[...], (((1,), (1,)), ((), ())), preferred_element_type=F32
    )
    rows = tok // n_col
    n_x = n_col // 2
    for j in range(n_x):
        for side in range(2):
            to_z = pos_ref[5] if side == 0 else 1 - pos_ref[5]
            to = to_z * n_x + lax.rem(pos_ref[4] + n_x - j, n_x)
            for t in range(2):
                first = t * tok + (2 * j + side) * rows
                send_ref[to, t] = acc_ref[pl.ds(first, rows), :].astype(BF16)


def down(pos, mask, parts, weight, n_col, width=512):
    n_row, _, share, depth = parts.shape
    feats = weight.shape[0]
    tok = share * n_row
    rows = tok // n_col
    return pl.pallas_call(
        functools.partial(down_kernel, n_col, n_row),
        grid=(feats // width,),
        in_specs=[SMEM_SPEC, SMEM_SPEC]
        + [pl.BlockSpec((n_row, 2, share, depth), lambda n: (0, 0, 0, 0))]
        + [pl.BlockSpec((width, depth), lambda n: (n, 0))],
        out_specs=pl.BlockSpec((n_col, 2, rows, width), lambda n: (0, 0, 0, n)),
        out_shape=jax.ShapeDtypeStruct((n_col, 2, rows, feats), BF16),
        scratch_shapes=[
            pltpu.VMEM((2 * tok, depth), BF16),
            pltpu.VMEM((width, depth), BF16),
            pltpu.VMEM((2 * tok, width), F32),
        ],
        cost_estimate=LONG,
        compiler_params=params(limit=WIDE_LIMIT),
        name="down",
    )(pos, mask, parts, pltpu.with_memory_space_constraint(weight, pltpu.HBM))


def grad_kernel(n_col, n_row, n_z, pos_ref, *refs):
    near, far = refs[:n_col], refs[n_col : 2 * n_col + 1]
    hidden = refs[2 * n_col + 1 : 2 * n_col + 1 + n_row]
    mine_ref, other_ref, x_ref, h_ref, sum_ref = refs[-5:]
    rows = near[0].shape[2]
    share = hidden[0].shape[2]
    tok = rows * 2 * n_col

    @pl.when(pl.program_id(0) == 0)
    def _():
        for k in range(n_row):
            owner = lax.rem(pos_ref[0] + n_row - k, n_row)
            for z in range(n_z):
                first = pl.multiple_of(z * tok + owner * share, share)
                for t in range(2):
                    h_ref[t, pl.ds(first, share), :] = hidden[k][z, t]

    for t in range(2):
        for j in range(n_col):
            for side in range(2):
                first = (2 * j + side) * rows
                x_ref[t, pl.ds(first, rows), :] = near[j][side, t]
                source = far[n_col if j == 2 and side == 1 else j]
                for z in range(1, n_z):
                    at = 0 if j == 2 else side
                    x_ref[t, pl.ds(z * tok + first, rows), :] = source[at, z - 1, t]
    over_tokens = (((0,), (0,)), ((), ()))
    total = lax.dot_general(x_ref[1], h_ref[0], over_tokens, preferred_element_type=F32)
    total += lax.dot_general(x_ref[0], h_ref[1], over_tokens, preferred_element_type=F32)
    sum_ref[...] = total
    mine = pl.multiple_of(pos_ref[2] * BLOCK, BLOCK)
    mine_ref[...] = sum_ref[:, pl.ds(mine, BLOCK)]
    other_ref[...] = sum_ref[:, pl.ds(BLOCK - mine, BLOCK)]


def grad(pos, near, far, hidden, width=512):
    n_col, n_row = len(near), len(hidden)
    _, _, rows, feats = near[0].shape
    n_z, _, share, cols = hidden[0].shape
    tok = n_z * rows * 2 * n_col
    return pl.pallas_call(
        functools.partial(grad_kernel, n_col, n_row, n_z),
        grid=(feats // width,),
        in_specs=[SMEM_SPEC]
        + [pl.BlockSpec((2, 2, rows, width), lambda n: (0, 0, 0, n))] * n_col
        + [
            pl.BlockSpec((f.shape[0], n_z - 1, 2, rows, width), lambda n: (0, 0, 0, 0, n))
            for f in far
        ]
        + [pl.BlockSpec((n_z, 2, share, cols), lambda n: (0, 0, 0, 0))] * n_row,
        out_specs=[pl.BlockSpec((width, BLOCK), lambda n: (n, 0))] * 2,
        out_shape=[jax.ShapeDtypeStruct((feats, BLOCK), F32)] * 2,
        scratch_shapes=[
            pltpu.VMEM((2, tok, width), BF16),
            pltpu.VMEM((2, tok, cols), BF16),
            pltpu.VMEM((width, cols), F32),
        ],
        cost_estimate=LONG,
        compiler_params=params(limit=WIDE_LIMIT),
        name="grad",
    )(pos, *near, *far, *hidden)


def finish_kernel(norm_scale, pos_ref, mask_ref, a_ref, b_ref, out_ref):
    blocks = a_ref.shape[0] // BLOCK
    for i in range(blocks):
        kept = mask_ref[pl.program_id(0) * blocks + i, pos_ref[3]] != 0
        part = pl.ds(i * BLOCK, BLOCK)
        total = (a_ref[part, :] + b_ref[part, :]) * norm_scale
        total = jnp.where(kept, total, jnp.zeros_like(total))
        out_ref[pl.ds(2 * i * BLOCK, BLOCK, 2), :] = total[:, :128]
        out_ref[pl.ds(2 * i * BLOCK + 1, BLOCK, 2), :] = total[:, 128:]


def finish(pos, mask, mine, theirs, norm_scale, height=1024):
    feats = mine.shape[0]
    block = pl.BlockSpec((height, BLOCK), lambda n: (n, 0))
    return pl.pallas_call(
        functools.partial(finish_kernel, norm_scale),
        grid=(feats // height,),
        in_specs=[SMEM_SPEC, SMEM_SPEC, block, block],
        out_specs=pl.BlockSpec((2 * height, 128), lambda n: (n, 0)),
        out_shape=jax.ShapeDtypeStruct((2 * feats, 128), F32),
        cost_estimate=COST,
        compiler_params=params(),
        name="finish",
    )(pos, mask, mine, theirs)


def on_device(tokens, cotangent, weight, block_mask):
    n_dp, n_row, n_col = (lax.axis_size(a) for a in ("dp", "row", "col"))
    n_z = n_dp // 2
    n_x = n_col // 2
    dp_at, col_at = lax.axis_index("dp"), lax.axis_index("col")
    pos = jnp.stack(
        [lax.axis_index("row"), dp_at // 2, dp_at % 2, dp_at, col_at % n_x, col_at // n_x]
    ).astype(jnp.int32)
    both = jnp.stack([tokens, cotangent])

    both, swapped = lax.optimization_barrier((both, shift_col(both, 0, 1)))
    pair = jnp.stack([both, swapped])
    near = [pair] + [shift_col(pair, j) for j in range(1, n_x)]
    far = [shift(both, "dp", 2 * k) for k in range(1, n_z)]

    own, *sends = up(pos, block_mask, near, weight, n_row)
    own, sends, far = lax.optimization_barrier((own, sends, far))
    far = jnp.stack(far)
    far_swap = shift_col(far, 0, 1)
    recv = [shift(s, "row", k + 1) for k, s in enumerate(sends)]
    far = jnp.stack([far, far_swap])
    own, far = lax.optimization_barrier((own, far))
    left, right = shift_col(far, 1), shift_col(far, -1)
    acts, *pieces = act(pos, own, recv, n_z)
    acts = lax.all_to_all(acts, "row", 0, 0)
    pieces = jnp.stack([pieces[0]] + [shift(pieces[k], "dp", 2 * k) for k in range(1, n_z)])
    pieces, left, right = lax.optimization_barrier((pieces, left, right))
    across = [shift_col(left[:1], 1), shift_col(right[1:], -1)]
    far = [far, left, across[0], right, across[1]]
    pieces_all = [pieces] + [shift(pieces, "row", k) for k in range(1, n_row)]

    sends = down(pos, block_mask, acts, weight, n_col)
    sends, near = lax.optimization_barrier((sends, near))
    total = lax.all_to_all(sends, "col", 0, 0).astype(F32).sum(axis=0) + both.astype(F32)
    output, input_grad = total[0].astype(BF16), total[1].astype(BF16)

    mine, given = grad(pos, near, far, pieces_all)
    theirs = lax.ppermute(given, "dp", [(i, i ^ 1) for i in range(n_dp)])
    tok_total = tokens.shape[0] * n_col * n_dp
    weight_grad = finish(pos, block_mask, mine, theirs, 1.0 / math.sqrt(tok_total))
    return output, input_grad, weight_grad.reshape(weight.shape[0], 1, BLOCK)


def solution(mesh):
    in_specs = (P(("dp", "col"), "row"), P(("dp", "col"), "row"), P("row", "col"), P("row", "col"))
    out_specs = (P(("dp", "col"), "row"), P(("dp", "col"), "row"), P("row", "dp", "col"))
    return jax.shard_map(
        on_device, mesh=mesh, in_specs=in_specs, out_specs=out_specs, check_vma=False
    )
```

```python
import functools
import math

import jax
import jax.numpy as jnp
from jax import lax
from jax.experimental import pallas as pl
from jax.experimental.pallas import tpu as pltpu
from jax.sharding import PartitionSpec as P

BLOCK = 256
VMEM_LIMIT = 24 * 1024 * 1024
WIDE_LIMIT = 56 * 1024 * 1024
SMEM_SPEC = pl.BlockSpec(memory_space=pltpu.SMEM)
COST = pl.CostEstimate(flops=1, bytes_accessed=1, transcendentals=0)
MEDIUM = pl.CostEstimate(flops=3000000000, bytes_accessed=1, transcendentals=0)
LONG = pl.CostEstimate(flops=100000000000, bytes_accessed=1000000000, transcendentals=0)
BF16, F32 = jnp.bfloat16, jnp.float32


def shift(value, axis, by):
    size = lax.axis_size(axis)
    return lax.ppermute(value, axis, [(i, (i + by) % size) for i in range(size)])


def shift_col(value, by_x, swap=0):
    half = lax.axis_size("col") // 2
    pairs = [(i, (i // half ^ swap) * half + (i + by_x) % half) for i in range(2 * half)]
    return lax.ppermute(value, "col", pairs)


def params(steps=1, limit=VMEM_LIMIT):
    return pltpu.CompilerParams(
        vmem_limit_bytes=limit, dimension_semantics=("arbitrary",) * steps
    )


def masked_copy(mask_ref, w_ref, out_ref, row0, col0):
    for i in range(w_ref.shape[0] // BLOCK):
        for j in range(w_ref.shape[1] // BLOCK):
            part = (pl.ds(i * BLOCK, BLOCK), pl.ds(j * BLOCK, BLOCK))
            kept = mask_ref[row0 + i, col0 + j] != 0
            out_ref[part] = jnp.where(kept, w_ref[part], jnp.zeros((BLOCK, BLOCK), BF16))


def up_kernel(n_col, n_row, pos_ref, mask_ref, *refs):
    parts, w_ref = refs[:n_col], refs[n_col]
    own_ref, sends = refs[n_col + 1], refs[n_col + 2 : n_col + 1 + n_row]
    x_ref, wm_ref, acc_ref = refs[-3:]
    rows = parts[0].shape[2]
    tok = rows * 2 * n_col
    step = pl.program_id(0)

    @pl.when(step == 0)
    def _():
        for t in range(2):
            for j in range(n_col):
                for side in range(2):
                    x_ref[pl.ds(t * tok + (2 * j + side) * rows, rows), :] = parts[j][side, t]

    masked_copy(mask_ref, w_ref, wm_ref, 0, step * (w_ref.shape[1] // BLOCK))
    acc_ref[...] = jnp.dot(x_ref[...], wm_ref[...], preferred_element_type=F32)
    share = tok // n_row
    me = pos_ref[0]
    for t in range(2):
        for k in range(n_row):
            first = pl.multiple_of(t * tok + lax.rem(me + k, n_row) * share, share)
            value = acc_ref[pl.ds(first, share), :]
            if k == 0:
                own_ref[t] = value
            else:
                sends[k - 1][t] = value.astype(BF16)


def up(pos, mask, parts, weight, n_row, width=512):
    n_col, (_, _, rows, depth) = len(parts), parts[0].shape
    cols = weight.shape[1]
    tok = rows * 2 * n_col
    share = tok // n_row
    return pl.pallas_call(
        functools.partial(up_kernel, n_col, n_row),
        grid=(cols // width,),
        in_specs=[SMEM_SPEC, SMEM_SPEC]
        + [pl.BlockSpec((2, 2, rows, depth), lambda n: (0, 0, 0, 0))] * n_col
        + [pl.BlockSpec((depth, width), lambda n: (0, n))],
        out_specs=[pl.BlockSpec((2, share, width), lambda n: (0, 0, n))] * n_row,
        out_shape=[jax.ShapeDtypeStruct((2, share, cols), F32)]
        + [jax.ShapeDtypeStruct((2, share, cols), BF16)] * (n_row - 1),
        scratch_shapes=[
            pltpu.VMEM((2 * tok, depth), BF16),
            pltpu.VMEM((depth, width), BF16),
            pltpu.VMEM((2 * tok, width), F32),
        ],
        cost_estimate=COST,
        compiler_params=params(),
        name="up",
    )(pos, mask, *parts, pltpu.with_memory_space_constraint(weight, pltpu.HBM))


def act_kernel(n_row, n_z, pos_ref, *refs):
    own_ref, recv = refs[0], refs[1:n_row]
    all_ref, pieces = refs[n_row], refs[n_row + 1 :]
    pre = own_ref[0]
    grad_hidden = own_ref[1]
    for ref in recv:
        pre = pre + ref[0].astype(F32)
        grad_hidden = grad_hidden + ref[1].astype(F32)
    sig = jax.nn.sigmoid(pre)
    all_ref[0, 0] = (pre * sig).astype(BF16)
    all_ref[0, 1] = (grad_hidden * sig * (1.0 + pre * (1.0 - sig))).astype(BF16)
    for r in range(1, n_row):
        all_ref[r] = all_ref[0]
    width = all_ref.shape[3] // n_z
    for k in range(n_z):
        first = pl.multiple_of(lax.rem(pos_ref[1] + k, n_z) * width, width)
        pieces[k][...] = all_ref[0, :, :, pl.ds(first, width)]


def act(pos, own, recv, n_z):
    _, share, cols = own.shape
    n_row = len(recv) + 1
    return pl.pallas_call(
        functools.partial(act_kernel, n_row, n_z),
        in_specs=[SMEM_SPEC] + [pl.BlockSpec(memory_space=pltpu.VMEM)] * n_row,
        out_specs=[pl.BlockSpec(memory_space=pltpu.VMEM)] * (n_z + 1),
        out_shape=[jax.ShapeDtypeStruct((n_row, 2, share, cols), BF16)]
        + [jax.ShapeDtypeStruct((2, share, cols // n_z), BF16)] * n_z,
        cost_estimate=COST,
        compiler_params=params(0),
        name="act",
    )(pos, own, *recv)


def down_kernel(n_col, n_row, pos_ref, mask_ref, *refs):
    parts_ref, w_ref, send_ref = refs[:3]
    x_ref, wm_ref, acc_ref = refs[-3:]
    share = parts_ref.shape[2]
    tok = share * n_row
    step = pl.program_id(0)

    @pl.when(step == 0)
    def _():
        for t in range(2):
            for r in range(n_row):
                x_ref[pl.ds(t * tok + r * share, share), :] = parts_ref[r, t]

    masked_copy(mask_ref, w_ref, wm_ref, step * (w_ref.shape[0] // BLOCK), 0)
    acc_ref[...] = lax.dot_general(
        x_ref[...], wm_ref[...], (((1,), (1,)), ((), ())), preferred_element_type=F32
    )
    rows = tok // n_col
    n_x = n_col // 2
    for j in range(n_x):
        for side in range(2):
            to_z = pos_ref[5] if side == 0 else 1 - pos_ref[5]
            to = to_z * n_x + lax.rem(pos_ref[4] + n_x - j, n_x)
            for t in range(2):
                first = t * tok + (2 * j + side) * rows
                send_ref[to, t] = acc_ref[pl.ds(first, rows), :].astype(BF16)


def down(pos, mask, parts, weight, n_col, width=512):
    n_row, _, share, depth = parts.shape
    feats = weight.shape[0]
    tok = share * n_row
    rows = tok // n_col
    return pl.pallas_call(
        functools.partial(down_kernel, n_col, n_row),
        grid=(feats // width,),
        in_specs=[SMEM_SPEC, SMEM_SPEC]
        + [pl.BlockSpec((n_row, 2, share, depth), lambda n: (0, 0, 0, 0))]
        + [pl.BlockSpec((width, depth), lambda n: (n, 0))],
        out_specs=pl.BlockSpec((n_col, 2, rows, width), lambda n: (0, 0, 0, n)),
        out_shape=jax.ShapeDtypeStruct((n_col, 2, rows, feats), BF16),
        scratch_shapes=[
            pltpu.VMEM((2 * tok, depth), BF16),
            pltpu.VMEM((width, depth), BF16),
            pltpu.VMEM((2 * tok, width), F32),
        ],
        cost_estimate=MEDIUM,
        compiler_params=params(limit=WIDE_LIMIT),
        name="down",
    )(pos, mask, parts, pltpu.with_memory_space_constraint(weight, pltpu.HBM))


def grad_kernel(n_col, n_row, n_z, pos_ref, *refs):
    near, far = refs[:n_col], refs[n_col : 2 * n_col + 1]
    hidden = refs[2 * n_col + 1 : 2 * n_col + 1 + n_row]
    mine_ref, other_ref, x_ref, h_ref, sum_ref = refs[-5:]
    rows = near[0].shape[2]
    share = hidden[0].shape[2]
    tok = rows * 2 * n_col

    @pl.when(pl.program_id(0) == 0)
    def _():
        for k in range(n_row):
            owner = lax.rem(pos_ref[0] + n_row - k, n_row)
            for z in range(n_z):
                first = pl.multiple_of(z * tok + owner * share, share)
                for t in range(2):
                    h_ref[t, pl.ds(first, share), :] = hidden[k][z, t]

    for t in range(2):
        for j in range(n_col):
            for side in range(2):
                first = (2 * j + side) * rows
                x_ref[t, pl.ds(first, rows), :] = near[j][side, t]
                source = far[n_col if j == 2 and side == 1 else j]
                for z in range(1, n_z):
                    at = 0 if j == 2 else side
                    x_ref[t, pl.ds(z * tok + first, rows), :] = source[at, z - 1, t]
    over_tokens = (((0,), (0,)), ((), ()))
    total = lax.dot_general(x_ref[1], h_ref[0], over_tokens, preferred_element_type=F32)
    total += lax.dot_general(x_ref[0], h_ref[1], over_tokens, preferred_element_type=F32)
    sum_ref[...] = total
    mine = pl.multiple_of(pos_ref[2] * BLOCK, BLOCK)
    mine_ref[...] = sum_ref[:, pl.ds(mine, BLOCK)]
    other_ref[...] = sum_ref[:, pl.ds(BLOCK - mine, BLOCK)]


def grad(pos, near, far, hidden, width=512):
    n_col, n_row = len(near), len(hidden)
    _, _, rows, feats = near[0].shape
    n_z, _, share, cols = hidden[0].shape
    tok = n_z * rows * 2 * n_col
    return pl.pallas_call(
        functools.partial(grad_kernel, n_col, n_row, n_z),
        grid=(feats // width,),
        in_specs=[SMEM_SPEC]
        + [pl.BlockSpec((2, 2, rows, width), lambda n: (0, 0, 0, n))] * n_col
        + [
            pl.BlockSpec((f.shape[0], n_z - 1, 2, rows, width), lambda n: (0, 0, 0, 0, n))
            for f in far
        ]
        + [pl.BlockSpec((n_z, 2, share, cols), lambda n: (0, 0, 0, 0))] * n_row,
        out_specs=[pl.BlockSpec((width, BLOCK), lambda n: (n, 0))] * 2,
        out_shape=[jax.ShapeDtypeStruct((feats, BLOCK), F32)] * 2,
        scratch_shapes=[
            pltpu.VMEM((2, tok, width), BF16),
            pltpu.VMEM((2, tok, cols), BF16),
            pltpu.VMEM((width, cols), F32),
        ],
        cost_estimate=LONG,
        compiler_params=params(limit=WIDE_LIMIT),
        name="grad",
    )(pos, *near, *far, *hidden)


def finish_kernel(norm_scale, pos_ref, mask_ref, a_ref, b_ref, out_ref):
    blocks = a_ref.shape[0] // BLOCK
    for i in range(blocks):
        kept = mask_ref[pl.program_id(0) * blocks + i, pos_ref[3]] != 0
        part = pl.ds(i * BLOCK, BLOCK)
        total = (a_ref[part, :] + b_ref[part, :]) * norm_scale
        total = jnp.where(kept, total, jnp.zeros_like(total))
        out_ref[pl.ds(2 * i * BLOCK, BLOCK, 2), :] = total[:, :128]
        out_ref[pl.ds(2 * i * BLOCK + 1, BLOCK, 2), :] = total[:, 128:]


def finish(pos, mask, mine, theirs, norm_scale, height=1024):
    feats = mine.shape[0]
    block = pl.BlockSpec((height, BLOCK), lambda n: (n, 0))
    return pl.pallas_call(
        functools.partial(finish_kernel, norm_scale),
        grid=(feats // height,),
        in_specs=[SMEM_SPEC, SMEM_SPEC, block, block],
        out_specs=pl.BlockSpec((2 * height, 128), lambda n: (n, 0)),
        out_shape=jax.ShapeDtypeStruct((2 * feats, 128), F32),
        cost_estimate=COST,
        compiler_params=params(),
        name="finish",
    )(pos, mask, mine, pltpu.with_memory_space_constraint(theirs, pltpu.HBM))


def add_kernel(sums_ref, tok_ref, cot_ref, *out_refs):
    for t, (first, out_ref) in enumerate(zip((tok_ref, cot_ref), out_refs)):
        total = first[...].astype(F32)
        for c in range(sums_ref.shape[0]):
            total = total + sums_ref[c, t].astype(F32)
        out_ref[...] = total.astype(BF16)


def add(sums, tokens, cotangent):
    return pl.pallas_call(
        add_kernel,
        in_specs=[pl.BlockSpec(memory_space=pltpu.VMEM)] * 3,
        out_specs=[pl.BlockSpec(memory_space=pltpu.VMEM)] * 2,
        out_shape=[jax.ShapeDtypeStruct(tokens.shape, BF16)] * 2,
        cost_estimate=COST,
        compiler_params=params(0),
        name="add",
    )(sums, tokens, cotangent)


def on_device(tokens, cotangent, weight, block_mask):
    n_dp, n_row, n_col = (lax.axis_size(a) for a in ("dp", "row", "col"))
    n_z = n_dp // 2
    n_x = n_col // 2
    dp_at, col_at = lax.axis_index("dp"), lax.axis_index("col")
    pos = jnp.stack(
        [lax.axis_index("row"), dp_at // 2, dp_at % 2, dp_at, col_at % n_x, col_at // n_x]
    ).astype(jnp.int32)
    both = jnp.stack([tokens, cotangent])

    both, swapped = lax.optimization_barrier((both, shift_col(both, 0, 1)))
    pair = jnp.stack([both, swapped])
    near = [pair] + [shift_col(pair, j) for j in range(1, n_x)]
    far = [shift(both, "dp", 2 * k) for k in range(1, n_z)]

    own, *sends = up(pos, block_mask, near, weight, n_row)
    own, sends, far = lax.optimization_barrier((own, sends, far))
    far = jnp.stack(far)
    far_swap = shift_col(far, 0, 1)
    recv = [shift(s, "row", k + 1) for k, s in enumerate(sends)]
    far = jnp.stack([far, far_swap])
    own, far = lax.optimization_barrier((own, far))
    left, right = shift_col(far, 1), shift_col(far, -1)
    acts, *pieces = act(pos, own, recv, n_z)
    acts = lax.all_to_all(acts, "row", 0, 0)
    pieces = jnp.stack([pieces[0]] + [shift(pieces[k], "dp", 2 * k) for k in range(1, n_z)])
    halves = (left[:1], right[1:])
    pieces, halves, left, right = lax.optimization_barrier((pieces, halves, left, right))
    across = [shift_col(halves[0], 1), shift_col(halves[1], -1)]
    far = [far, left, across[0], right, across[1]]
    pieces_all = [pieces] + [shift(pieces, "row", k) for k in range(1, n_row)]

    sends = down(pos, block_mask, acts, weight, n_col)
    sends, near = lax.optimization_barrier((sends, near))
    output, input_grad = add(lax.all_to_all(sends, "col", 0, 0), tokens, cotangent)

    mine, given = grad(pos, near, far, pieces_all)
    theirs = lax.ppermute(given, "dp", [(i, i ^ 1) for i in range(n_dp)])
    tok_total = tokens.shape[0] * n_col * n_dp
    weight_grad = finish(pos, block_mask, mine, theirs, 1.0 / math.sqrt(tok_total))
    return output, input_grad, weight_grad.reshape(weight.shape[0], 1, BLOCK)


def solution(mesh):
    in_specs = (P(("dp", "col"), "row"), P(("dp", "col"), "row"), P("row", "col"), P("row", "col"))
    out_specs = (P(("dp", "col"), "row"), P(("dp", "col"), "row"), P("row", "dp", "col"))
    return jax.shard_map(
        on_device, mesh=mesh, in_specs=in_specs, out_specs=out_specs, check_vma=False
    )
```

```python
import functools
import math

import jax
import jax.numpy as jnp
from jax import lax
from jax.experimental import pallas as pl
from jax.experimental.pallas import tpu as pltpu
from jax.sharding import PartitionSpec as P

BLOCK = 256
VMEM_LIMIT = 24 * 1024 * 1024
WIDE_LIMIT = 56 * 1024 * 1024
SMEM_SPEC = pl.BlockSpec(memory_space=pltpu.SMEM)
COST = pl.CostEstimate(flops=1, bytes_accessed=1, transcendentals=0)
MEDIUM = pl.CostEstimate(flops=6000000000, bytes_accessed=1, transcendentals=0)
LONG = pl.CostEstimate(flops=100000000000, bytes_accessed=1000000000, transcendentals=0)
BF16, F32 = jnp.bfloat16, jnp.float32


def shift(value, axis, by):
    size = lax.axis_size(axis)
    return lax.ppermute(value, axis, [(i, (i + by) % size) for i in range(size)])


def shift_col(value, by_x, swap=0):
    half = lax.axis_size("col") // 2
    pairs = [(i, (i // half ^ swap) * half + (i + by_x) % half) for i in range(2 * half)]
    return lax.ppermute(value, "col", pairs)


def params(steps=1, limit=VMEM_LIMIT):
    return pltpu.CompilerParams(
        vmem_limit_bytes=limit, dimension_semantics=("arbitrary",) * steps
    )


def masked_copy(mask_ref, w_ref, out_ref, row0, col0):
    for i in range(w_ref.shape[0] // BLOCK):
        for j in range(w_ref.shape[1] // BLOCK):
            part = (pl.ds(i * BLOCK, BLOCK), pl.ds(j * BLOCK, BLOCK))
            kept = mask_ref[row0 + i, col0 + j] != 0
            out_ref[part] = jnp.where(kept, w_ref[part], jnp.zeros((BLOCK, BLOCK), BF16))


def up_kernel(n_col, n_row, pos_ref, mask_ref, *refs):
    parts, w_ref = refs[:n_col], refs[n_col]
    own_ref, sends = refs[n_col + 1], refs[n_col + 2 : n_col + 1 + n_row]
    x_ref, wm_ref, acc_ref = refs[-3:]
    rows = parts[0].shape[2]
    tok = rows * 2 * n_col
    step = pl.program_id(0)

    @pl.when(step == 0)
    def _():
        for t in range(2):
            for j in range(n_col):
                for side in range(2):
                    x_ref[pl.ds(t * tok + (2 * j + side) * rows, rows), :] = parts[j][side, t]

    masked_copy(mask_ref, w_ref, wm_ref, 0, step * (w_ref.shape[1] // BLOCK))
    acc_ref[...] = jnp.dot(x_ref[...], wm_ref[...], preferred_element_type=F32)
    share = tok // n_row
    me = pos_ref[0]
    for t in range(2):
        for k in range(n_row):
            first = pl.multiple_of(t * tok + lax.rem(me + k, n_row) * share, share)
            value = acc_ref[pl.ds(first, share), :]
            if k == 0:
                own_ref[t] = value
            else:
                sends[k - 1][t] = value.astype(BF16)


def up(pos, mask, parts, weight, n_row, width=512):
    n_col, (_, _, rows, depth) = len(parts), parts[0].shape
    cols = weight.shape[1]
    tok = rows * 2 * n_col
    share = tok // n_row
    return pl.pallas_call(
        functools.partial(up_kernel, n_col, n_row),
        grid=(cols // width,),
        in_specs=[SMEM_SPEC, SMEM_SPEC]
        + [pl.BlockSpec((2, 2, rows, depth), lambda n: (0, 0, 0, 0))] * n_col
        + [pl.BlockSpec((depth, width), lambda n: (0, n))],
        out_specs=[pl.BlockSpec((2, share, width), lambda n: (0, 0, n))] * n_row,
        out_shape=[jax.ShapeDtypeStruct((2, share, cols), F32)]
        + [jax.ShapeDtypeStruct((2, share, cols), BF16)] * (n_row - 1),
        scratch_shapes=[
            pltpu.VMEM((2 * tok, depth), BF16),
            pltpu.VMEM((depth, width), BF16),
            pltpu.VMEM((2 * tok, width), F32),
        ],
        cost_estimate=COST,
        compiler_params=params(),
        name="up",
    )(pos, mask, *parts, pltpu.with_memory_space_constraint(weight, pltpu.HBM))


def act_kernel(n_row, n_z, pos_ref, *refs):
    own_ref, recv = refs[0], refs[1:n_row]
    all_ref, pieces = refs[n_row], refs[n_row + 1 :]
    pre = own_ref[0]
    grad_hidden = own_ref[1]
    for ref in recv:
        pre = pre + ref[0].astype(F32)
        grad_hidden = grad_hidden + ref[1].astype(F32)
    sig = jax.nn.sigmoid(pre)
    all_ref[0, 0] = (pre * sig).astype(BF16)
    all_ref[0, 1] = (grad_hidden * sig * (1.0 + pre * (1.0 - sig))).astype(BF16)
    for r in range(1, n_row):
        all_ref[r] = all_ref[0]
    width = all_ref.shape[3] // n_z
    for k in range(n_z):
        first = pl.multiple_of(lax.rem(pos_ref[1] + k, n_z) * width, width)
        pieces[k][...] = all_ref[0, :, :, pl.ds(first, width)]


def act(pos, own, recv, n_z):
    _, share, cols = own.shape
    n_row = len(recv) + 1
    return pl.pallas_call(
        functools.partial(act_kernel, n_row, n_z),
        in_specs=[SMEM_SPEC] + [pl.BlockSpec(memory_space=pltpu.VMEM)] * n_row,
        out_specs=[pl.BlockSpec(memory_space=pltpu.VMEM)] * (n_z + 1),
        out_shape=[jax.ShapeDtypeStruct((n_row, 2, share, cols), BF16)]
        + [jax.ShapeDtypeStruct((2, share, cols // n_z), BF16)] * n_z,
        cost_estimate=COST,
        compiler_params=params(0),
        name="act",
    )(pos, own, *recv)


def down_kernel(n_col, n_row, pos_ref, mask_ref, *refs):
    parts_ref, w_ref, send_ref = refs[:3]
    x_ref, wm_ref, acc_ref = refs[-3:]
    share = parts_ref.shape[2]
    tok = share * n_row
    step = pl.program_id(0)

    @pl.when(step == 0)
    def _():
        for t in range(2):
            for r in range(n_row):
                x_ref[pl.ds(t * tok + r * share, share), :] = parts_ref[r, t]

    masked_copy(mask_ref, w_ref, wm_ref, step * (w_ref.shape[0] // BLOCK), 0)
    acc_ref[...] = lax.dot_general(
        x_ref[...], wm_ref[...], (((1,), (1,)), ((), ())), preferred_element_type=F32
    )
    rows = tok // n_col
    n_x = n_col // 2
    for j in range(n_x):
        for side in range(2):
            to_z = pos_ref[5] if side == 0 else 1 - pos_ref[5]
            to = to_z * n_x + lax.rem(pos_ref[4] + n_x - j, n_x)
            for t in range(2):
                first = t * tok + (2 * j + side) * rows
                send_ref[to, t] = acc_ref[pl.ds(first, rows), :].astype(BF16)


def down(pos, mask, parts, weight, n_col, width=512):
    n_row, _, share, depth = parts.shape
    feats = weight.shape[0]
    tok = share * n_row
    rows = tok // n_col
    return pl.pallas_call(
        functools.partial(down_kernel, n_col, n_row),
        grid=(feats // width,),
        in_specs=[SMEM_SPEC, SMEM_SPEC]
        + [pl.BlockSpec((n_row, 2, share, depth), lambda n: (0, 0, 0, 0))]
        + [pl.BlockSpec((width, depth), lambda n: (n, 0))],
        out_specs=pl.BlockSpec((n_col, 2, rows, width), lambda n: (0, 0, 0, n)),
        out_shape=jax.ShapeDtypeStruct((n_col, 2, rows, feats), BF16),
        scratch_shapes=[
            pltpu.VMEM((2 * tok, depth), BF16),
            pltpu.VMEM((width, depth), BF16),
            pltpu.VMEM((2 * tok, width), F32),
        ],
        cost_estimate=MEDIUM,
        compiler_params=params(limit=WIDE_LIMIT),
        name="down",
    )(pos, mask, parts, pltpu.with_memory_space_constraint(weight, pltpu.HBM))


def grad_kernel(n_col, n_row, n_z, pos_ref, *refs):
    near, far = refs[:n_col], refs[n_col : 2 * n_col + 1]
    hidden = refs[2 * n_col + 1 : 2 * n_col + 1 + n_row]
    mine_ref, other_ref, x_ref, h_ref, sum_ref = refs[-5:]
    rows = near[0].shape[2]
    share = hidden[0].shape[2]
    tok = rows * 2 * n_col

    @pl.when(pl.program_id(0) == 0)
    def _():
        for k in range(n_row):
            owner = lax.rem(pos_ref[0] + n_row - k, n_row)
            for z in range(n_z):
                first = pl.multiple_of(z * tok + owner * share, share)
                for t in range(2):
                    h_ref[t, pl.ds(first, share), :] = hidden[k][z, t]

    for t in range(2):
        for j in range(n_col):
            for side in range(2):
                first = (2 * j + side) * rows
                x_ref[t, pl.ds(first, rows), :] = near[j][side, t]
                source = far[n_col if j == 2 and side == 1 else j]
                for z in range(1, n_z):
                    at = 0 if j == 2 else side
                    x_ref[t, pl.ds(z * tok + first, rows), :] = source[at, z - 1, t]
    over_tokens = (((0,), (0,)), ((), ()))
    total = lax.dot_general(x_ref[1], h_ref[0], over_tokens, preferred_element_type=F32)
    total += lax.dot_general(x_ref[0], h_ref[1], over_tokens, preferred_element_type=F32)
    sum_ref[...] = total
    mine = pl.multiple_of(pos_ref[2] * BLOCK, BLOCK)
    mine_ref[...] = sum_ref[:, pl.ds(mine, BLOCK)]
    other_ref[...] = sum_ref[:, pl.ds(BLOCK - mine, BLOCK)]


def grad(pos, near, far, hidden, width=512):
    n_col, n_row = len(near), len(hidden)
    _, _, rows, feats = near[0].shape
    n_z, _, share, cols = hidden[0].shape
    tok = n_z * rows * 2 * n_col
    return pl.pallas_call(
        functools.partial(grad_kernel, n_col, n_row, n_z),
        grid=(feats // width,),
        in_specs=[SMEM_SPEC]
        + [pl.BlockSpec((2, 2, rows, width), lambda n: (0, 0, 0, n))] * n_col
        + [
            pl.BlockSpec((f.shape[0], n_z - 1, 2, rows, width), lambda n: (0, 0, 0, 0, n))
            for f in far
        ]
        + [pl.BlockSpec((n_z, 2, share, cols), lambda n: (0, 0, 0, 0))] * n_row,
        out_specs=[pl.BlockSpec((width, BLOCK), lambda n: (n, 0))] * 2,
        out_shape=[jax.ShapeDtypeStruct((feats, BLOCK), F32)] * 2,
        scratch_shapes=[
            pltpu.VMEM((2, tok, width), BF16),
            pltpu.VMEM((2, tok, cols), BF16),
            pltpu.VMEM((width, cols), F32),
        ],
        cost_estimate=LONG,
        compiler_params=params(limit=WIDE_LIMIT),
        name="grad",
    )(pos, *near, *far, *hidden)


def finish_kernel(norm_scale, pos_ref, mask_ref, a_ref, b_ref, out_ref):
    blocks = a_ref.shape[0] // BLOCK
    for i in range(blocks):
        kept = mask_ref[pl.program_id(0) * blocks + i, pos_ref[3]] != 0
        part = pl.ds(i * BLOCK, BLOCK)
        total = (a_ref[part, :] + b_ref[part, :]) * norm_scale
        total = jnp.where(kept, total, jnp.zeros_like(total))
        out_ref[pl.ds(2 * i * BLOCK, BLOCK, 2), :] = total[:, :128]
        out_ref[pl.ds(2 * i * BLOCK + 1, BLOCK, 2), :] = total[:, 128:]


def finish(pos, mask, mine, theirs, norm_scale, height=1024):
    feats = mine.shape[0]
    block = pl.BlockSpec((height, BLOCK), lambda n: (n, 0))
    return pl.pallas_call(
        functools.partial(finish_kernel, norm_scale),
        grid=(feats // height,),
        in_specs=[SMEM_SPEC, SMEM_SPEC, block, block],
        out_specs=pl.BlockSpec((2 * height, 128), lambda n: (n, 0)),
        out_shape=jax.ShapeDtypeStruct((2 * feats, 128), F32),
        cost_estimate=COST,
        compiler_params=params(),
        name="finish",
    )(pos, mask, mine, theirs)


def add_kernel(sums_ref, tok_ref, cot_ref, *out_refs):
    for t, (first, out_ref) in enumerate(zip((tok_ref, cot_ref), out_refs)):
        total = first[...].astype(F32)
        for c in range(sums_ref.shape[0]):
            total = total + sums_ref[c, t].astype(F32)
        out_ref[...] = total.astype(BF16)


def add(sums, tokens, cotangent):
    return pl.pallas_call(
        add_kernel,
        in_specs=[pl.BlockSpec(memory_space=pltpu.VMEM)] * 3,
        out_specs=[pl.BlockSpec(memory_space=pltpu.VMEM)] * 2,
        out_shape=[jax.ShapeDtypeStruct(tokens.shape, BF16)] * 2,
        cost_estimate=COST,
        compiler_params=params(0),
        name="add",
    )(sums, tokens, cotangent)


def on_device(tokens, cotangent, weight, block_mask):
    n_dp, n_row, n_col = (lax.axis_size(a) for a in ("dp", "row", "col"))
    n_z = n_dp // 2
    n_x = n_col // 2
    dp_at, col_at = lax.axis_index("dp"), lax.axis_index("col")
    pos = jnp.stack(
        [lax.axis_index("row"), dp_at // 2, dp_at % 2, dp_at, col_at % n_x, col_at // n_x]
    ).astype(jnp.int32)
    both = jnp.stack([tokens, cotangent])

    both, swapped = lax.optimization_barrier((both, shift_col(both, 0, 1)))
    pair = jnp.stack([both, swapped])
    near = [pair] + [shift_col(pair, j) for j in range(1, n_x)]
    far = [shift(both, "dp", 2 * k) for k in range(1, n_z)]

    own, *sends = up(pos, block_mask, near, weight, n_row)
    own, sends, far = lax.optimization_barrier((own, sends, far))
    far = jnp.stack(far)
    far_swap = shift_col(far, 0, 1)
    recv = [shift(s, "row", k + 1) for k, s in enumerate(sends)]
    far = jnp.stack([far, far_swap])
    own, far = lax.optimization_barrier((own, far))
    left, right = shift_col(far, 1), shift_col(far, -1)
    acts, *pieces = act(pos, own, recv, n_z)
    acts = lax.all_to_all(acts, "row", 0, 0)
    pieces = jnp.stack([pieces[0]] + [shift(pieces[k], "dp", 2 * k) for k in range(1, n_z)])
    halves = (left[:1], right[1:])
    across = [shift_col(halves[0], 1), shift_col(halves[1], -1)]
    far = [far, left, across[0], right, across[1]]
    pieces_all = [pieces] + [shift(pieces, "row", k) for k in range(1, n_row)]

    sends = down(pos, block_mask, acts, weight, n_col)
    sends, near = lax.optimization_barrier((sends, near))
    output, input_grad = add(lax.all_to_all(sends, "col", 0, 0), tokens, cotangent)

    mine, given = grad(pos, near, far, pieces_all)
    theirs = lax.ppermute(given, "dp", [(i, i ^ 1) for i in range(n_dp)])
    tok_total = tokens.shape[0] * n_col * n_dp
    weight_grad = finish(pos, block_mask, mine, theirs, 1.0 / math.sqrt(tok_total))
    return output, input_grad, weight_grad.reshape(weight.shape[0], 1, BLOCK)


def solution(mesh):
    in_specs = (P(("dp", "col"), "row"), P(("dp", "col"), "row"), P("row", "col"), P("row", "col"))
    out_specs = (P(("dp", "col"), "row"), P(("dp", "col"), "row"), P("row", "dp", "col"))
    return jax.shard_map(
        on_device, mesh=mesh, in_specs=in_specs, out_specs=out_specs, check_vma=False
    )
```

```python
import functools
import math

import jax
import jax.numpy as jnp
from jax import lax
from jax.experimental import pallas as pl
from jax.experimental.pallas import tpu as pltpu
from jax.sharding import PartitionSpec as P

BLOCK = 256
VMEM_LIMIT = 24 * 1024 * 1024
WIDE_LIMIT = 56 * 1024 * 1024
SMEM_SPEC = pl.BlockSpec(memory_space=pltpu.SMEM)
COST = pl.CostEstimate(flops=1, bytes_accessed=1, transcendentals=0)
MEDIUM = pl.CostEstimate(flops=6000000000, bytes_accessed=1, transcendentals=0)
LONG = pl.CostEstimate(flops=100000000000, bytes_accessed=1000000000, transcendentals=0)
BF16, F32 = jnp.bfloat16, jnp.float32


def shift(value, axis, by):
    size = lax.axis_size(axis)
    return lax.ppermute(value, axis, [(i, (i + by) % size) for i in range(size)])


def shift_col(value, by_x, swap=0):
    half = lax.axis_size("col") // 2
    pairs = [(i, (i // half ^ swap) * half + (i + by_x) % half) for i in range(2 * half)]
    return lax.ppermute(value, "col", pairs)


def params(steps=1, limit=VMEM_LIMIT):
    return pltpu.CompilerParams(
        vmem_limit_bytes=limit, dimension_semantics=("arbitrary",) * steps
    )


def masked_copy(mask_ref, w_ref, out_ref, row0, col0):
    for i in range(w_ref.shape[0] // BLOCK):
        for j in range(w_ref.shape[1] // BLOCK):
            part = (pl.ds(i * BLOCK, BLOCK), pl.ds(j * BLOCK, BLOCK))
            kept = mask_ref[row0 + i, col0 + j] != 0
            out_ref[part] = jnp.where(kept, w_ref[part], jnp.zeros((BLOCK, BLOCK), BF16))


def up_kernel(n_col, n_row, pos_ref, mask_ref, *refs):
    parts, w_ref = refs[:n_col], refs[n_col]
    own_ref, sends = refs[n_col + 1], refs[n_col + 2 : n_col + 1 + n_row]
    x_ref, wm_ref, acc_ref = refs[-3:]
    rows = parts[0].shape[2]
    tok = rows * 2 * n_col
    step = pl.program_id(0)

    @pl.when(step == 0)
    def _():
        for t in range(2):
            for j in range(n_col):
                for side in range(2):
                    x_ref[pl.ds(t * tok + (2 * j + side) * rows, rows), :] = parts[j][side, t]

    masked_copy(mask_ref, w_ref, wm_ref, 0, step * (w_ref.shape[1] // BLOCK))
    acc_ref[...] = jnp.dot(x_ref[...], wm_ref[...], preferred_element_type=F32)
    share = tok // n_row
    me = pos_ref[0]
    for t in range(2):
        for k in range(n_row):
            first = pl.multiple_of(t * tok + lax.rem(me + k, n_row) * share, share)
            value = acc_ref[pl.ds(first, share), :]
            if k == 0:
                own_ref[t] = value
            else:
                sends[k - 1][t] = value.astype(BF16)


def up(pos, mask, parts, weight, n_row, width=512):
    n_col, (_, _, rows, depth) = len(parts), parts[0].shape
    cols = weight.shape[1]
    tok = rows * 2 * n_col
    share = tok // n_row
    return pl.pallas_call(
        functools.partial(up_kernel, n_col, n_row),
        grid=(cols // width,),
        in_specs=[SMEM_SPEC, SMEM_SPEC]
        + [pl.BlockSpec((2, 2, rows, depth), lambda n: (0, 0, 0, 0))] * n_col
        + [pl.BlockSpec((depth, width), lambda n: (0, n))],
        out_specs=[pl.BlockSpec((2, share, width), lambda n: (0, 0, n))] * n_row,
        out_shape=[jax.ShapeDtypeStruct((2, share, cols), F32)]
        + [jax.ShapeDtypeStruct((2, share, cols), BF16)] * (n_row - 1),
        scratch_shapes=[
            pltpu.VMEM((2 * tok, depth), BF16),
            pltpu.VMEM((depth, width), BF16),
            pltpu.VMEM((2 * tok, width), F32),
        ],
        cost_estimate=COST,
        compiler_params=params(),
        name="up",
    )(pos, mask, *parts, pltpu.with_memory_space_constraint(weight, pltpu.HBM))


def act_kernel(n_row, n_z, pos_ref, *refs):
    own_ref, recv = refs[0], refs[1:n_row]
    all_ref, pieces = refs[n_row], refs[n_row + 1 :]
    pre = own_ref[0]
    grad_hidden = own_ref[1]
    for ref in recv:
        pre = pre + ref[0].astype(F32)
        grad_hidden = grad_hidden + ref[1].astype(F32)
    sig = jax.nn.sigmoid(pre)
    all_ref[0, 0] = (pre * sig).astype(BF16)
    all_ref[0, 1] = (grad_hidden * sig * (1.0 + pre * (1.0 - sig))).astype(BF16)
    for r in range(1, n_row):
        all_ref[r] = all_ref[0]
    width = all_ref.shape[3] // n_z
    for k in range(n_z):
        first = pl.multiple_of(lax.rem(pos_ref[1] + k, n_z) * width, width)
        pieces[k][...] = all_ref[0, :, :, pl.ds(first, width)]


def act(pos, own, recv, n_z):
    _, share, cols = own.shape
    n_row = len(recv) + 1
    return pl.pallas_call(
        functools.partial(act_kernel, n_row, n_z),
        in_specs=[SMEM_SPEC] + [pl.BlockSpec(memory_space=pltpu.VMEM)] * n_row,
        out_specs=[pl.BlockSpec(memory_space=pltpu.VMEM)] * (n_z + 1),
        out_shape=[jax.ShapeDtypeStruct((n_row, 2, share, cols), BF16)]
        + [jax.ShapeDtypeStruct((2, share, cols // n_z), BF16)] * n_z,
        cost_estimate=COST,
        compiler_params=params(0),
        name="act",
    )(pos, own, *recv)


def down_kernel(n_col, n_row, pos_ref, mask_ref, *refs):
    parts_ref, w_ref, send_ref = refs[:3]
    x_ref, wm_ref, acc_ref = refs[-3:]
    share = parts_ref.shape[2]
    tok = share * n_row
    step = pl.program_id(0)

    @pl.when(step == 0)
    def _():
        for t in range(2):
            for r in range(n_row):
                x_ref[pl.ds(t * tok + r * share, share), :] = parts_ref[r, t]

    masked_copy(mask_ref, w_ref, wm_ref, step * (w_ref.shape[0] // BLOCK), 0)
    acc_ref[...] = lax.dot_general(
        x_ref[...], wm_ref[...], (((1,), (1,)), ((), ())), preferred_element_type=F32
    )
    rows = tok // n_col
    n_x = n_col // 2
    for j in range(n_x):
        for side in range(2):
            to_z = pos_ref[5] if side == 0 else 1 - pos_ref[5]
            to = to_z * n_x + lax.rem(pos_ref[4] + n_x - j, n_x)
            for t in range(2):
                first = t * tok + (2 * j + side) * rows
                send_ref[to, t] = acc_ref[pl.ds(first, rows), :].astype(BF16)


def down(pos, mask, parts, weight, n_col, width=512):
    n_row, _, share, depth = parts.shape
    feats = weight.shape[0]
    tok = share * n_row
    rows = tok // n_col
    return pl.pallas_call(
        functools.partial(down_kernel, n_col, n_row),
        grid=(feats // width,),
        in_specs=[SMEM_SPEC, SMEM_SPEC]
        + [pl.BlockSpec((n_row, 2, share, depth), lambda n: (0, 0, 0, 0))]
        + [pl.BlockSpec((width, depth), lambda n: (n, 0))],
        out_specs=pl.BlockSpec((n_col, 2, rows, width), lambda n: (0, 0, 0, n)),
        out_shape=jax.ShapeDtypeStruct((n_col, 2, rows, feats), BF16),
        scratch_shapes=[
            pltpu.VMEM((2 * tok, depth), BF16),
            pltpu.VMEM((width, depth), BF16),
            pltpu.VMEM((2 * tok, width), F32),
        ],
        cost_estimate=MEDIUM,
        compiler_params=params(limit=WIDE_LIMIT),
        name="down",
    )(pos, mask, parts, pltpu.with_memory_space_constraint(weight, pltpu.HBM))


def grad_kernel(n_col, n_row, n_z, pos_ref, *refs):
    near, far = refs[:n_col], refs[n_col : 2 * n_col + 1]
    hidden = refs[2 * n_col + 1 : 2 * n_col + 1 + n_row]
    mine_ref, other_ref, x_ref, h_ref, sum_ref = refs[-5:]
    rows = near[0].shape[2]
    share = hidden[0].shape[2]
    tok = rows * 2 * n_col

    @pl.when(pl.program_id(0) == 0)
    def _():
        for k in range(n_row):
            owner = lax.rem(pos_ref[0] + n_row - k, n_row)
            for z in range(n_z):
                first = pl.multiple_of(z * tok + owner * share, share)
                for t in range(2):
                    h_ref[t, pl.ds(first, share), :] = hidden[k][z, t]

    for t in range(2):
        for j in range(n_col):
            for side in range(2):
                first = (2 * j + side) * rows
                x_ref[t, pl.ds(first, rows), :] = near[j][side, t]
                source = far[n_col if j == 2 and side == 1 else j]
                for z in range(1, n_z):
                    at = 0 if j == 2 else side
                    x_ref[t, pl.ds(z * tok + first, rows), :] = source[at, z - 1, t]
    over_tokens = (((0,), (0,)), ((), ()))
    total = lax.dot_general(x_ref[1], h_ref[0], over_tokens, preferred_element_type=F32)
    total += lax.dot_general(x_ref[0], h_ref[1], over_tokens, preferred_element_type=F32)
    sum_ref[...] = total
    mine = pl.multiple_of(pos_ref[2] * BLOCK, BLOCK)
    mine_ref[...] = sum_ref[:, pl.ds(mine, BLOCK)]
    other_ref[...] = sum_ref[:, pl.ds(BLOCK - mine, BLOCK)]


def grad(pos, near, far, hidden, width=1024):
    n_col, n_row = len(near), len(hidden)
    _, _, rows, feats = near[0].shape
    n_z, _, share, cols = hidden[0].shape
    tok = n_z * rows * 2 * n_col
    return pl.pallas_call(
        functools.partial(grad_kernel, n_col, n_row, n_z),
        grid=(feats // width,),
        in_specs=[SMEM_SPEC]
        + [pl.BlockSpec((2, 2, rows, width), lambda n: (0, 0, 0, n))] * n_col
        + [
            pl.BlockSpec((f.shape[0], n_z - 1, 2, rows, width), lambda n: (0, 0, 0, 0, n))
            for f in far
        ]
        + [pl.BlockSpec((n_z, 2, share, cols), lambda n: (0, 0, 0, 0))] * n_row,
        out_specs=[pl.BlockSpec((width, BLOCK), lambda n: (n, 0))] * 2,
        out_shape=[jax.ShapeDtypeStruct((feats, BLOCK), F32)] * 2,
        scratch_shapes=[
            pltpu.VMEM((2, tok, width), BF16),
            pltpu.VMEM((2, tok, cols), BF16),
            pltpu.VMEM((width, cols), F32),
        ],
        cost_estimate=LONG,
        compiler_params=params(limit=WIDE_LIMIT),
        name="grad",
    )(pos, *near, *far, *hidden)


def finish_kernel(norm_scale, pos_ref, mask_ref, a_ref, b_ref, out_ref):
    blocks = a_ref.shape[0] // BLOCK
    for i in range(blocks):
        kept = mask_ref[pl.program_id(0) * blocks + i, pos_ref[3]] != 0
        part = pl.ds(i * BLOCK, BLOCK)
        total = (a_ref[part, :] + b_ref[part, :]) * norm_scale
        total = jnp.where(kept, total, jnp.zeros_like(total))
        out_ref[pl.ds(2 * i * BLOCK, BLOCK, 2), :] = total[:, :128]
        out_ref[pl.ds(2 * i * BLOCK + 1, BLOCK, 2), :] = total[:, 128:]


def finish(pos, mask, mine, theirs, norm_scale, height=1024):
    feats = mine.shape[0]
    block = pl.BlockSpec((height, BLOCK), lambda n: (n, 0))
    return pl.pallas_call(
        functools.partial(finish_kernel, norm_scale),
        grid=(feats // height,),
        in_specs=[SMEM_SPEC, SMEM_SPEC, block, block],
        out_specs=pl.BlockSpec((2 * height, 128), lambda n: (n, 0)),
        out_shape=jax.ShapeDtypeStruct((2 * feats, 128), F32),
        cost_estimate=COST,
        compiler_params=params(),
        name="finish",
    )(pos, mask, mine, theirs)


def add_kernel(sums_ref, tok_ref, cot_ref, *out_refs):
    for t, (first, out_ref) in enumerate(zip((tok_ref, cot_ref), out_refs)):
        total = first[...].astype(F32)
        for c in range(sums_ref.shape[0]):
            total = total + sums_ref[c, t].astype(F32)
        out_ref[...] = total.astype(BF16)


def add(sums, tokens, cotangent):
    return pl.pallas_call(
        add_kernel,
        in_specs=[pl.BlockSpec(memory_space=pltpu.VMEM)] * 3,
        out_specs=[pl.BlockSpec(memory_space=pltpu.VMEM)] * 2,
        out_shape=[jax.ShapeDtypeStruct(tokens.shape, BF16)] * 2,
        cost_estimate=COST,
        compiler_params=params(0),
        name="add",
    )(sums, tokens, cotangent)


def on_device(tokens, cotangent, weight, block_mask):
    n_dp, n_row, n_col = (lax.axis_size(a) for a in ("dp", "row", "col"))
    n_z = n_dp // 2
    n_x = n_col // 2
    dp_at, col_at = lax.axis_index("dp"), lax.axis_index("col")
    pos = jnp.stack(
        [lax.axis_index("row"), dp_at // 2, dp_at % 2, dp_at, col_at % n_x, col_at // n_x]
    ).astype(jnp.int32)
    both = jnp.stack([tokens, cotangent])

    both, swapped = lax.optimization_barrier((both, shift_col(both, 0, 1)))
    pair = jnp.stack([both, swapped])
    near = [pair] + [shift_col(pair, j) for j in range(1, n_x)]
    far = [shift(both, "dp", 2 * k) for k in range(1, n_z)]

    own, *sends = up(pos, block_mask, near, weight, n_row)
    own, sends, far = lax.optimization_barrier((own, sends, far))
    far = jnp.stack(far)
    far_swap = shift_col(far, 0, 1)
    recv = [shift(s, "row", k + 1) for k, s in enumerate(sends)]
    far = jnp.stack([far, far_swap])
    own, far = lax.optimization_barrier((own, far))
    left, right = shift_col(far, 1), shift_col(far, -1)
    acts, *pieces = act(pos, own, recv, n_z)
    acts = lax.all_to_all(acts, "row", 0, 0)
    pieces = jnp.stack([pieces[0]] + [shift(pieces[k], "dp", 2 * k) for k in range(1, n_z)])
    halves = (left[:1], right[1:])
    across = [shift_col(halves[0], 1), shift_col(halves[1], -1)]
    far = [far, left, across[0], right, across[1]]
    pieces_all = [pieces] + [shift(pieces, "row", k) for k in range(1, n_row)]

    sends = down(pos, block_mask, acts, weight, n_col)
    sends, near = lax.optimization_barrier((sends, near))
    output, input_grad = add(lax.all_to_all(sends, "col", 0, 0), tokens, cotangent)

    mine, given = grad(pos, near, far, pieces_all)
    theirs = lax.ppermute(given, "dp", [(i, i ^ 1) for i in range(n_dp)])
    tok_total = tokens.shape[0] * n_col * n_dp
    weight_grad = finish(pos, block_mask, mine, theirs, 1.0 / math.sqrt(tok_total))
    return output, input_grad, weight_grad.reshape(weight.shape[0], 1, BLOCK)


def solution(mesh):
    in_specs = (P(("dp", "col"), "row"), P(("dp", "col"), "row"), P("row", "col"), P("row", "col"))
    out_specs = (P(("dp", "col"), "row"), P(("dp", "col"), "row"), P("row", "dp", "col"))
    return jax.shard_map(
        on_device, mesh=mesh, in_specs=in_specs, out_specs=out_specs, check_vma=False
    )
```
